512 devices in a mesh: phys: 2 (over x_hi), gx: 16 (over z), gy: 16 (over x_lo, y, core).
Axes of the slice: x: 4 (x_hi: 2, x_lo: 2; x = x_hi * 2 + x_lo), y: 4, z: 16, core: 2. Of those that a mesh axis runs over, the one named last changes fastest.
Arguments:
- models: float32 [2, 4, 1024, 2048], P('phys', None, 'gx', 'gy'), may hold values from -6 to 6
- channel_weight: float32 [2, 6], replicated, may hold values from 50 to 500
Outputs:
- gradient: float32 [2, 4, 1024, 2048], P('phys', None, 'gx', 'gy')
The draws below stay inside these ranges and needn't reach their ends.
All inputs are finite; a program needn't handle non-finite values.
Results may differ from the reference program's by a relative error of at most 0.0001.
Values sent between devices are 32-bit elements; how exact they have to be, the bound alone decides.
No kernel may reach another device: no remote copies, remote signals or barrier semaphores. Data moves between devices by JAX's collectives and lax.ppermute only.
A program may use at most 64 MiB of HBM per device.

```python
import math
import jax
import jax.numpy as jnp
from jax import lax

Z = 4
NX = 1024
NY = 2048


def levels(key, dims, split, least, top_value):
    factor_of, own = 1.0, jax.random.fold_in(key, 6)
    for dim, blocks in split:
        draws = jnp.exp(jax.random.uniform(jax.random.fold_in(own, dim), (blocks,), jnp.float32, least / len(split), top_value / len(split)))
        factor_of = factor_of * jnp.repeat(draws, dims[dim] // blocks).reshape([-1 if axis == dim else 1 for axis in range(len(dims))])
    return factor_of


def scatter_about(key, shape, width, reach, cuts=(), held_as=jnp.bfloat16):
    level = levels(key, shape, cuts, -0.22, 0.18) if cuts else 1.0
    drawn = jax.random.normal(key, shape, jnp.float32) * width * level
    return jnp.minimum(jnp.maximum(drawn, -reach), reach).astype(held_as)


def setup_inputs(seed: int = 0) -> dict:
    key_list = jax.random.split(jax.random.key(seed), 3)
    models = scatter_about(key_list[0], (2, Z, NX, NY), 1.0, 6.0, ((0, 2), (2, 16), (3, 16)), jnp.float32)
    channel_weight = jnp.clip(jnp.exp(jax.random.uniform(key_list[1], (2, 6), jnp.float32, math.log(50.0), math.log(500.0))), 50.0, 500.0)
    return {"models": models, "channel_weight": channel_weight}


gauss_total = sum(math.exp(-j * j / 50.0) for j in range(-15, 16))


def kernel_matrix(rows_n, cols_n, offset, dilation):
    row_index = lax.broadcasted_iota(jnp.int32, (rows_n, cols_n), 0)
    col_index = lax.broadcasted_iota(jnp.int32, (rows_n, cols_n), 1)
    distance = row_index - col_index + offset
    tap_index = distance // dilation
    on_tap = (distance == tap_index * dilation) & (jnp.abs(tap_index) <= 15)
    tap_float = tap_index.astype(jnp.float32)
    weights = jnp.exp(-tap_float * tap_float / 50.0) / gauss_total
    return jnp.where(on_tap, weights, 0.0).astype(jnp.float32)


def smooth_middle(values, dilation):
    lead, length, trail = values.shape
    highest = lax.Precision.HIGHEST
    if length <= 256:
        return jnp.einsum('ij,ajb->aib', kernel_matrix(length, length, 0, dilation), values, precision=highest)
    block_count = length // 128
    blocks = values.reshape(lead, block_count, 128, trail)
    zero_block = jnp.zeros((lead, 1, 128, trail), values.dtype)
    after_blocks = jnp.concatenate([blocks[:, 1:], zero_block], 1)
    before_blocks = jnp.concatenate([zero_block, blocks[:, :-1]], 1)
    result = jnp.einsum('ij,anjb->anib', kernel_matrix(128, 128, 0, dilation), blocks, precision=highest)
    result = result + jnp.einsum('ij,anjb->anib', kernel_matrix(128, 128, -128, dilation), after_blocks, precision=highest)
    result = result + jnp.einsum('ij,anjb->anib', kernel_matrix(128, 128, 128, dilation), before_blocks, precision=highest)
    return result.reshape(lead, length, trail)


def smooth_last(values, dilation):
    lead, trail, length = values.shape
    highest = lax.Precision.HIGHEST
    if length <= 256:
        return jnp.einsum('ajk,ik->aji', values, kernel_matrix(length, length, 0, dilation), precision=highest)
    block_count = length // 128
    blocks = values.reshape(lead, trail, block_count, 128)
    zero_block = jnp.zeros((lead, trail, 1, 128), values.dtype)
    after_blocks = jnp.concatenate([blocks[:, :, 1:], zero_block], 2)
    before_blocks = jnp.concatenate([zero_block, blocks[:, :, :-1]], 2)
    result = jnp.einsum('ajnk,ik->ajni', blocks, kernel_matrix(128, 128, 0, dilation), precision=highest)
    result = result + jnp.einsum('ajnk,ik->ajni', after_blocks, kernel_matrix(128, 128, -128, dilation), precision=highest)
    result = result + jnp.einsum('ajnk,ik->ajni', before_blocks, kernel_matrix(128, 128, 128, dilation), precision=highest)
    return result.reshape(lead, trail, length)


def smooth_all(row_stack):
    row_count, x_cells, y_cells = row_stack.shape
    half_rows = row_count // 2
    depth_cells = row_count // 12
    z_rows = row_stack.reshape(12, depth_cells, x_cells * y_cells)
    z_done = jnp.concatenate([smooth_middle(z_rows[:6], 1), smooth_middle(z_rows[6:], 4)], 0)
    z_done = z_done.reshape(row_count, x_cells, y_cells)
    x_done = jnp.concatenate([smooth_middle(z_done[:half_rows], 1), smooth_middle(z_done[half_rows:], 4)], 0)
    return jnp.concatenate([smooth_last(x_done[:half_rows], 1), smooth_last(x_done[half_rows:], 4)], 0)


def slopes(model_field):
    padded = jnp.pad(model_field, 1)
    slope_x = 0.5 * (padded[1:-1, 2:, 1:-1] - padded[1:-1, :-2, 1:-1])
    slope_y = 0.5 * (padded[1:-1, 1:-1, 2:] - padded[1:-1, 1:-1, :-2])
    slope_z = 0.5 * (padded[2:, 1:-1, 1:-1] - padded[:-2, 1:-1, 1:-1])
    return slope_x, slope_y, slope_z


def reference(models, channel_weight):
    weights = jnp.repeat(channel_weight.reshape(12), Z)[:, None, None]
    slope_list = []
    smoothed_list = []
    for which in range(2):
        slope_x, slope_y, slope_z = slopes(models[which])
        tensor = jnp.stack([slope_x * slope_x, slope_y * slope_y, slope_z * slope_z,
                            slope_x * slope_y, slope_x * slope_z, slope_y * slope_z], 0)
        row_stack = jnp.concatenate([tensor, tensor], 0).reshape(12 * Z, NX, NY)
        smoothed_list.append(smooth_all(row_stack))
        slope_list.append((slope_x, slope_y, slope_z))
    outputs = []
    for which in range(2):
        slope_x, slope_y, slope_z = slope_list[which]
        weighted = (smoothed_list[which] - smoothed_list[1 - which]) * weights
        adjoint = smooth_all(weighted)
        combined = (adjoint[:6 * Z] + adjoint[6 * Z:]).reshape(6, Z, NX, NY)
        q_x = 2.0 * combined[0] * slope_x + combined[3] * slope_y + combined[4] * slope_z
        q_y = 2.0 * combined[1] * slope_y + combined[3] * slope_x + combined[5] * slope_z
        q_z = 2.0 * combined[2] * slope_z + combined[4] * slope_x + combined[5] * slope_y
        pad_x = jnp.pad(q_x, 1)
        pad_y = jnp.pad(q_y, 1)
        pad_z = jnp.pad(q_z, 1)
        result = 0.5 * (pad_x[1:-1, :-2, 1:-1] - pad_x[1:-1, 2:, 1:-1])
        result = result + 0.5 * (pad_y[1:-1, 1:-1, :-2] - pad_y[1:-1, 1:-1, 2:])
        result = result + 0.5 * (pad_z[:-2, 1:-1, 1:-1] - pad_z[2:, 1:-1, 1:-1])
        outputs.append(result)
    return jnp.stack(outputs, 0)
```

```python
import math

import jax
import jax.numpy as jnp
import ml_dtypes
import numpy as np
from jax import lax
from jax.experimental import pallas as pl
from jax.experimental.pallas import tpu as pltpu
from jax.sharding import PartitionSpec as P

DILATIONS = (1, 4)
TAPS = 15
LANES = 128
ROWS = 80
KEPT = 72


def taps():
    weights = np.array([math.exp(-k * k / 50.0) for k in range(-TAPS, TAPS + 1)])
    return weights / weights.sum()


def squared(length, dilation):
    matrix = np.zeros((length, length))
    for k, weight in zip(range(-TAPS, TAPS + 1), taps()):
        matrix += weight * np.eye(length, k=dilation * k)
    return matrix @ matrix


def window(matrix, row_ids, col_ids):
    count = matrix.shape[0]
    row_ok = (row_ids >= 0) & (row_ids < count)
    col_ok = (col_ids >= 0) & (col_ids < count)
    picked = matrix[np.clip(row_ids, 0, count - 1)][:, np.clip(col_ids, 0, count - 1)]
    return picked * row_ok[:, None] * col_ok[None, :]


def chosen(tables, index):
    distinct, place = np.unique(tables, axis=0, return_inverse=True)
    high = distinct.astype(np.float32).astype(ml_dtypes.bfloat16)
    low = (distinct - high.astype(np.float64)).astype(np.float32).astype(ml_dtypes.bfloat16)
    which = jnp.asarray(place.reshape(-1).astype(np.int32))[index]
    return [lax.dynamic_index_in_dim(jnp.asarray(t), which, 0, False) for t in (high, low)]


def split_f32(value):
    high = value.astype(jnp.bfloat16)
    low = (value - high.astype(jnp.float32)).astype(jnp.bfloat16)
    return high, low


def off_grid(count):
    return np.full(count, -1)


def x_tables(peers, block):
    tables = []
    matrices = [squared(peers * block, d) for d in DILATIONS]
    for i in range(peers):
        start = i * block
        out_ids = np.concatenate(
            [
                np.arange(start, start + block + 1),
                off_grid(KEPT - block - 2),
                [start - 1],
                off_grid(ROWS - KEPT),
            ]
        )
        in_ids = np.arange(start - 2 * block, start + 3 * block)
        tables.append(np.concatenate([window(m, out_ids, in_ids) for m in matrices], 0))
    return np.stack(tables)


def y_tables(peers, block):
    tables = []
    fine, coarse = [squared(peers * block, d) for d in DILATIONS]
    for i in range(peers):
        start = i * block
        own = np.arange(start, start + block)
        left, right = own - block, own + block
        edge = np.concatenate([right[: block // 2], left[block // 2 :]])
        out_ids = np.concatenate(
            [own, [start + block], off_grid(block - 2), [start - 1]]
        )
        wide = np.concatenate([left, own, right])
        near = np.concatenate([own, edge])
        tables.append(
            np.concatenate(
                [window(coarse, out_ids, wide).T, window(fine, out_ids, near).T], 0
            )
        )
    return np.stack(tables)


def lane_index(shape):
    return lax.broadcasted_iota(jnp.int32, shape, len(shape) - 1)


def pack_kernel(ext_ref, left_ref, right_ref, out_ref):
    block = out_ref.shape[1] - 8
    start = 2 * block
    for z in range(out_ref.shape[0]):
        for column in range(2):
            def rows(at, count):
                if column == 0:
                    return ext_ref[z, at : at + count, :]
                l = left_ref[z, at : at + count, :]
                r = right_ref[z, at : at + count, :]
                return jnp.where(lane_index(l.shape) < LANES // 2, r, l)

            after, before = rows(start + block, 8), rows(start - 8, 8)
            sub = lax.broadcasted_iota(jnp.int32, after.shape, 0)
            lanes = slice(column * LANES, (column + 1) * LANES)
            out_ref[z, 0:block, lanes] = rows(start, block)
            out_ref[z, block : block + 8, lanes] = jnp.where(sub < 4, after, before)


def smooth_kernel(
    depth_w, weight_ref, ext_ref, left_ref, right_ref, xh_ref, xl_ref, yh_ref, yl_ref,
    out_ref, slope_ref, near_ref, high_ref, low_ref,
):
    depth, rows, _ = ext_ref.shape
    blocks = (left_ref, ext_ref, right_ref)
    chunk = 32
    centre = float(depth_w[1][0][0])

    x_both = jnp.concatenate([xh_ref[...], xl_ref[...]], 0)
    x_high = xh_ref[...]
    for pair in range(depth // 2):
        for k in range(2):
            z = 2 * pair + k
            for b in range(3):
                lanes = slice((3 * k + b) * LANES, (3 * k + b + 1) * LANES)
                for r in range(0, rows, chunk):
                    at = slice(r, r + chunk)
                    mid = blocks[b][z, at, :]
                    if r == 0:
                        before = jnp.concatenate([mid[:1], mid[:-1]], 0)
                    else:
                        before = blocks[b][z, r - 1 : r + chunk - 1, :]
                    if r + chunk == rows:
                        after = jnp.concatenate([mid[1:], mid[-1:]], 0)
                    else:
                        after = blocks[b][z, r + 1 : r + chunk + 1, :]
                    slope_ref[0, at, lanes] = 0.5 * (after - before)
                    lane = lane_index(mid.shape)
                    prev, nxt = pltpu.roll(mid, 1, 1), pltpu.roll(mid, LANES - 1, 1)
                    if b > 0:
                        prev = jnp.where(lane == 0, pltpu.roll(blocks[b - 1][z, at, :], 1, 1), prev)
                    if b < 2:
                        nxt = jnp.where(
                            lane == LANES - 1, pltpu.roll(blocks[b + 1][z, at, :], LANES - 1, 1), nxt
                        )
                    slope_ref[1, at, lanes] = 0.5 * (nxt - prev)
                    above = blocks[b][z + 1, at, :] if z + 1 < depth else jnp.zeros_like(mid)
                    below = blocks[b][z - 1, at, :] if z > 0 else jnp.zeros_like(mid)
                    slope_ref[2, at, lanes] = 0.5 * (above - below)
        for c, (i, j) in enumerate(((0, 0), (1, 1), (2, 2), (0, 1), (0, 2), (1, 2))):
            high, low = split_f32(slope_ref[i] * slope_ref[j])
            first = jnp.dot(x_both, high, preferred_element_type=jnp.float32)
            second = jnp.dot(x_high, low, preferred_element_type=jnp.float32)
            done = first[: 2 * ROWS] + first[2 * ROWS :] + second
            fine, coarse = done[:ROWS], done[ROWS:]
            scale = weight_ref[1, c] * centre
            for k in range(2):
                z = 2 * pair + k
                at = slice((c * depth + z) * ROWS, (c * depth + z + 1) * ROWS)
                wide = coarse[:, 3 * k * LANES : 3 * (k + 1) * LANES] * scale
                high_ref[at, : 3 * LANES], low_ref[at, : 3 * LANES] = split_f32(wide)
                l, o, r = [
                    fine[:, (3 * k + b) * LANES : (3 * k + b + 1) * LANES] for b in range(3)
                ]
                near_ref[c, z, :, :LANES] = o
                near_ref[c, z, :, LANES:] = jnp.where(lane_index(l.shape) < LANES // 2, r, l)
    for c in range(6):
        for z in range(depth):
            mixed = near_ref[c, 0] * (weight_ref[0, c] * float(depth_w[0][z][0]))
            for k in range(1, depth):
                mixed = mixed + near_ref[c, k] * (weight_ref[0, c] * float(depth_w[0][z][k]))
            at = slice((c * depth + z) * ROWS, (c * depth + z + 1) * ROWS)
            high_ref[at, 3 * LANES :], low_ref[at, 3 * LANES :] = split_f32(mixed)
    for c in range(6):
        at = slice(c * depth * ROWS, (c + 1) * depth * ROWS)
        high, low = high_ref[at, :], low_ref[at, :]
        done = jnp.dot(high, yh_ref[...], preferred_element_type=jnp.float32)
        done = done + jnp.dot(low, yh_ref[...], preferred_element_type=jnp.float32)
        done = done + jnp.dot(high, yl_ref[...], preferred_element_type=jnp.float32)
        for z in range(depth):
            out_ref[c, z] = done[z * ROWS : z * ROWS + KEPT]


def gradient_kernel(adj_ref, mine_ref, other_ref, own_ref, send_ref):
    depth, rows, cols = mine_ref.shape
    block = own_ref.shape[1]
    for model, result, sign in ((mine_ref, own_ref, 0.5), (other_ref, send_ref, -0.5)):
        q_z = []
        total = []
        for z in range(depth):
            m = model[z]
            s_x = 0.5 * (pltpu.roll(m, rows - 1, 0) - pltpu.roll(m, 1, 0))
            s_y = 0.5 * (pltpu.roll(m, cols - 1, 1) - pltpu.roll(m, 1, 1))
            above = model[z + 1] if z + 1 < depth else jnp.zeros_like(m)
            below = model[z - 1] if z > 0 else jnp.zeros_like(m)
            s_z = 0.5 * (above - below)
            a = [adj_ref[c, z] for c in range(6)]
            q_x = 2.0 * a[0] * s_x + a[3] * s_y + a[4] * s_z
            q_y = 2.0 * a[1] * s_y + a[3] * s_x + a[5] * s_z
            q_z.append((2.0 * a[2] * s_z + a[4] * s_x + a[5] * s_y)[:block, :LANES])
            lateral = pltpu.roll(q_x, 1, 0) - pltpu.roll(q_x, rows - 1, 0)
            lateral = lateral + pltpu.roll(q_y, 1, 1) - pltpu.roll(q_y, cols - 1, 1)
            total.append(lateral[:block, :LANES])
        for z in range(depth):
            value = total[z]
            if z > 0:
                value = value + q_z[z - 1]
            if z + 1 < depth:
                value = value - q_z[z + 1]
            result[z] = sign * value


def shift(value, axis, step):
    peers = lax.axis_size(axis)
    route = [(i, i + step) for i in range(peers) if 0 <= i + step < peers]
    return lax.ppermute(value, axis, route)


def solution(mesh):
    x_peers, y_peers = mesh.shape["gx"], mesh.shape["gy"]

    def shards(models, channel_weight):
        field = models[0]
        depth, x_cells, y_cells = field.shape
        depth_w = [squared(depth, d).tolist() for d in DILATIONS]
        x_index, y_index = lax.axis_index("gx"), lax.axis_index("gy")
        x_high, x_low = chosen(x_tables(x_peers, x_cells), x_index)
        y_high, y_low = chosen(y_tables(y_peers, y_cells), y_index)
        near = [shift(field, "gx", 1), shift(field, "gx", -1)]
        far = [shift(field, "gx", 2), shift(field, "gx", -2)]
        ext = jnp.concatenate([far[0], near[0], field, near[1], far[1]], 1)
        left, right = shift(ext, "gy", 1), shift(ext, "gy", -1)
        vmem = pl.BlockSpec(memory_space=pltpu.VMEM)
        smem = pl.BlockSpec(memory_space=pltpu.SMEM)
        params = pltpu.CompilerParams(vmem_limit_bytes=48 * 1024 * 1024)
        f32 = jnp.float32
        mine = pl.pallas_call(
            pack_kernel,
            out_shape=jax.ShapeDtypeStruct((depth, KEPT, 2 * LANES), f32),
            in_specs=[vmem] * 3,
            out_specs=vmem,
            compiler_params=params,
        )(ext, left, right)
        other = lax.ppermute(mine, "phys", [(0, 1), (1, 0)])
        rows = 5 * x_cells
        adjoint = pl.pallas_call(
            lambda *refs: smooth_kernel(depth_w, *refs),
            out_shape=jax.ShapeDtypeStruct((6, depth, KEPT, 2 * LANES), f32),
            in_specs=[smem] + [vmem] * 7,
            out_specs=vmem,
            scratch_shapes=[
                pltpu.VMEM((3, rows, 6 * LANES), f32),
                pltpu.VMEM((6, depth, ROWS, 2 * LANES), f32),
                pltpu.VMEM((6 * depth * ROWS, 5 * LANES), jnp.bfloat16),
                pltpu.VMEM((6 * depth * ROWS, 5 * LANES), jnp.bfloat16),
            ],
            compiler_params=params,
            cost_estimate=pl.CostEstimate(
                flops=8 * 10**9, bytes_accessed=4 * 10**6, transcendentals=0
            ),
        )(channel_weight, ext, left, right, x_high, x_low, y_high, y_low)
        own, send = pl.pallas_call(
            gradient_kernel,
            out_shape=[jax.ShapeDtypeStruct(field.shape, f32)] * 2,
            in_specs=[vmem] * 3,
            out_specs=[vmem] * 2,
            compiler_params=params,
        )(adjoint, mine, other)
        got = lax.ppermute(send, "phys", [(0, 1), (1, 0)])
        return (own + got)[None]

    in_specs = (P("phys", None, "gx", "gy"), P())
    out_specs = P("phys", None, "gx", "gy")
    return jax.shard_map(shards, mesh=mesh, in_specs=in_specs, out_specs=out_specs, check_vma=False)
```

```python
import math

import jax
import jax.numpy as jnp
import ml_dtypes
import numpy as np
from jax import lax
from jax.experimental import pallas as pl
from jax.experimental.pallas import tpu as pltpu
from jax.sharding import PartitionSpec as P

DILATIONS = (1, 4)
TAPS = 15
LANES = 128
ROWS = 80
KEPT = 72


def taps():
    weights = np.array([math.exp(-k * k / 50.0) for k in range(-TAPS, TAPS + 1)])
    return weights / weights.sum()


def squared(length, dilation):
    matrix = np.zeros((length, length))
    for k, weight in zip(range(-TAPS, TAPS + 1), taps()):
        matrix += weight * np.eye(length, k=dilation * k)
    return matrix @ matrix


def window(matrix, row_ids, col_ids):
    count = matrix.shape[0]
    row_ok = (row_ids >= 0) & (row_ids < count)
    col_ok = (col_ids >= 0) & (col_ids < count)
    picked = matrix[np.clip(row_ids, 0, count - 1)][:, np.clip(col_ids, 0, count - 1)]
    return picked * row_ok[:, None] * col_ok[None, :]


def stored(tables, edge):
    count = tables.shape[0]
    if count > 2 * edge + 1:
        tables = np.concatenate([tables[: edge + 1], tables[count - edge :]], 0)
    high = tables.astype(np.float32).astype(ml_dtypes.bfloat16)
    low = (tables - high.astype(np.float64)).astype(np.float32).astype(ml_dtypes.bfloat16)
    return jnp.asarray(np.stack([high, low], 1))


def table_of(index, count, edge):
    if count <= 2 * edge + 1:
        return index
    return jnp.minimum(index, edge) + jnp.maximum(index - (count - 1 - edge), 0)


def split_f32(value):
    high = value.astype(jnp.bfloat16)
    low = (value - high.astype(jnp.float32)).astype(jnp.bfloat16)
    return high, low


def off_grid(count):
    return np.full(count, -1)


def x_tables(peers, block):
    tables = []
    matrices = [squared(peers * block, d) for d in DILATIONS]
    for i in range(peers):
        start = i * block
        out_ids = np.concatenate(
            [
                np.arange(start, start + block + 1),
                off_grid(KEPT - block - 2),
                [start - 1],
                off_grid(ROWS - KEPT),
            ]
        )
        in_ids = np.arange(start - 2 * block, start + 3 * block)
        tables.append(np.concatenate([window(m, out_ids, in_ids) for m in matrices], 0))
    return np.stack(tables)


def y_tables(peers, block):
    tables = []
    fine, coarse = [squared(peers * block, d) for d in DILATIONS]
    for i in range(peers):
        start = i * block
        own = np.arange(start, start + block)
        left, right = own - block, own + block
        edge = np.concatenate([right[: block // 2], left[block // 2 :]])
        out_ids = np.concatenate(
            [own, [start + block], off_grid(block - 2), [start - 1]]
        )
        wide = np.concatenate([left, own, right])
        near = np.concatenate([own, edge])
        tables.append(
            np.concatenate(
                [window(coarse, out_ids, wide).T, window(fine, out_ids, near).T], 0
            )
        )
    return np.stack(tables)


def lane_index(shape):
    return lax.broadcasted_iota(jnp.int32, shape, len(shape) - 1)


def pack_kernel(near_ref, left_ref, right_ref, out_ref):
    block = out_ref.shape[1] - 8
    for z in range(out_ref.shape[0]):
        for column in range(2):
            def rows(at, count):
                if column == 0:
                    return near_ref[z, at : at + count, :]
                l = left_ref[z, at : at + count, :]
                r = right_ref[z, at : at + count, :]
                return jnp.where(lane_index(l.shape) < LANES // 2, r, l)

            after, before = rows(2 * block, 8), rows(block - 8, 8)
            sub = lax.broadcasted_iota(jnp.int32, after.shape, 0)
            lanes = slice(column * LANES, (column + 1) * LANES)
            out_ref[z, 0:block, lanes] = rows(block, block)
            out_ref[z, block : block + 8, lanes] = jnp.where(sub < 4, after, before)


def smooth_kernel(
    depth_w, counts, which_ref, weight_ref, *refs
):
    inner_refs, outer_refs, refs = refs[:3], refs[3:6], refs[6:]
    x_all, y_all, out_ref, slope_ref, near_ref, high_ref, low_ref, ext_ref, x_ref, y_ref, x_sem, y_sem = refs
    blocks, depth, rows, _ = ext_ref.shape
    chunk = 32
    x_copy = pltpu.make_async_copy(x_all.at[table_of(which_ref[0], counts[0], 2)], x_ref, x_sem)
    y_copy = pltpu.make_async_copy(y_all.at[table_of(which_ref[1], counts[1], 1)], y_ref, y_sem)
    x_copy.start()
    y_copy.start()
    side = rows // 5
    for b in range(blocks):
        for z in range(depth):
            ext_ref[b, z, side : 4 * side] = inner_refs[b][z]
            ext_ref[b, z, :side] = outer_refs[b][z, :side]
            ext_ref[b, z, 4 * side :] = outer_refs[b][z, side:]
    x_copy.wait()
    centre = float(depth_w[1][0][0])

    x_both = jnp.concatenate([x_ref[0], x_ref[1]], 0)
    x_high = x_ref[0]
    for pair in range(depth // 2):
        for k in range(2):
            z = 2 * pair + k
            for b in range(3):
                lanes = slice((3 * k + b) * LANES, (3 * k + b + 1) * LANES)
                for r in range(0, rows, chunk):
                    at = slice(r, r + chunk)
                    mid = ext_ref[b, z, at, :]
                    if r == 0:
                        before = jnp.concatenate([mid[:1], mid[:-1]], 0)
                    else:
                        before = ext_ref[b, z, r - 1 : r + chunk - 1, :]
                    if r + chunk == rows:
                        after = jnp.concatenate([mid[1:], mid[-1:]], 0)
                    else:
                        after = ext_ref[b, z, r + 1 : r + chunk + 1, :]
                    slope_ref[0, at, lanes] = 0.5 * (after - before)
                    lane = lane_index(mid.shape)
                    prev, nxt = pltpu.roll(mid, 1, 1), pltpu.roll(mid, LANES - 1, 1)
                    if b > 0:
                        prev = jnp.where(lane == 0, pltpu.roll(ext_ref[b - 1, z, at, :], 1, 1), prev)
                    if b < 2:
                        nxt = jnp.where(
                            lane == LANES - 1, pltpu.roll(ext_ref[b + 1, z, at, :], LANES - 1, 1), nxt
                        )
                    slope_ref[1, at, lanes] = 0.5 * (nxt - prev)
                    above = ext_ref[b, z + 1, at, :] if z + 1 < depth else jnp.zeros_like(mid)
                    below = ext_ref[b, z - 1, at, :] if z > 0 else jnp.zeros_like(mid)
                    slope_ref[2, at, lanes] = 0.5 * (above - below)
        for c, (i, j) in enumerate(((0, 0), (1, 1), (2, 2), (0, 1), (0, 2), (1, 2))):
            high, low = split_f32(slope_ref[i] * slope_ref[j])
            first = jnp.dot(x_both, high, preferred_element_type=jnp.float32)
            second = jnp.dot(x_high, low, preferred_element_type=jnp.float32)
            done = first[: 2 * ROWS] + first[2 * ROWS :] + second
            fine, coarse = done[:ROWS], done[ROWS:]
            scale = weight_ref[1, c] * centre
            for k in range(2):
                z = 2 * pair + k
                at = slice((c * depth + z) * ROWS, (c * depth + z + 1) * ROWS)
                wide = coarse[:, 3 * k * LANES : 3 * (k + 1) * LANES] * scale
                high_ref[at, : 3 * LANES], low_ref[at, : 3 * LANES] = split_f32(wide)
                l, o, r = [
                    fine[:, (3 * k + b) * LANES : (3 * k + b + 1) * LANES] for b in range(3)
                ]
                near_ref[c, z, :, :LANES] = o
                near_ref[c, z, :, LANES:] = jnp.where(lane_index(l.shape) < LANES // 2, r, l)
    for c in range(6):
        for z in range(depth):
            mixed = near_ref[c, 0] * (weight_ref[0, c] * float(depth_w[0][z][0]))
            for k in range(1, depth):
                mixed = mixed + near_ref[c, k] * (weight_ref[0, c] * float(depth_w[0][z][k]))
            at = slice((c * depth + z) * ROWS, (c * depth + z + 1) * ROWS)
            high_ref[at, 3 * LANES :], low_ref[at, 3 * LANES :] = split_f32(mixed)
    y_copy.wait()
    for c in range(6):
        at = slice(c * depth * ROWS, (c + 1) * depth * ROWS)
        high, low = high_ref[at, :], low_ref[at, :]
        done = jnp.dot(high, y_ref[0], preferred_element_type=jnp.float32)
        done = done + jnp.dot(low, y_ref[0], preferred_element_type=jnp.float32)
        done = done + jnp.dot(high, y_ref[1], preferred_element_type=jnp.float32)
        for z in range(depth):
            out_ref[c, z] = done[z * ROWS : z * ROWS + KEPT]


def gradient_kernel(adj_ref, mine_ref, other_ref, own_ref, send_ref):
    depth, rows, cols = mine_ref.shape
    block = own_ref.shape[1]
    for model, result, sign in ((mine_ref, own_ref, 0.5), (other_ref, send_ref, -0.5)):
        q_z = []
        total = []
        for z in range(depth):
            m = model[z]
            s_x = 0.5 * (pltpu.roll(m, rows - 1, 0) - pltpu.roll(m, 1, 0))
            s_y = 0.5 * (pltpu.roll(m, cols - 1, 1) - pltpu.roll(m, 1, 1))
            above = model[z + 1] if z + 1 < depth else jnp.zeros_like(m)
            below = model[z - 1] if z > 0 else jnp.zeros_like(m)
            s_z = 0.5 * (above - below)
            a = [adj_ref[c, z] for c in range(6)]
            q_x = 2.0 * a[0] * s_x + a[3] * s_y + a[4] * s_z
            q_y = 2.0 * a[1] * s_y + a[3] * s_x + a[5] * s_z
            q_z.append((2.0 * a[2] * s_z + a[4] * s_x + a[5] * s_y)[:block, :LANES])
            lateral = pltpu.roll(q_x, 1, 0) - pltpu.roll(q_x, rows - 1, 0)
            lateral = lateral + pltpu.roll(q_y, 1, 1) - pltpu.roll(q_y, cols - 1, 1)
            total.append(lateral[:block, :LANES])
        for z in range(depth):
            value = total[z]
            if z > 0:
                value = value + q_z[z - 1]
            if z + 1 < depth:
                value = value - q_z[z + 1]
            result[z] = sign * value


def shift(value, axis, step):
    peers = lax.axis_size(axis)
    route = [(i, i + step) for i in range(peers) if 0 <= i + step < peers]
    return lax.ppermute(value, axis, route)


def solution(mesh):
    x_peers, y_peers = mesh.shape["gx"], mesh.shape["gy"]

    def shards(models, channel_weight):
        field = models[0]
        depth, x_cells, y_cells = field.shape
        depth_w = [squared(depth, d).tolist() for d in DILATIONS]
        x_index, y_index = lax.axis_index("gx"), lax.axis_index("gy")
        x_all = stored(x_tables(x_peers, x_cells), 2)
        y_all = stored(y_tables(y_peers, y_cells), 1)
        which = jnp.stack([x_index, y_index])
        near = [shift(field, "gx", 1), shift(field, "gx", -1)]
        far = [shift(field, "gx", 2), shift(field, "gx", -2)]
        inner = jnp.concatenate([near[0], field, near[1]], 1)
        inner_sides = [shift(inner, "gy", 1), shift(inner, "gy", -1)]
        outer = jnp.concatenate(far, 1)
        outer_sides = [shift(outer, "gy", 1), shift(outer, "gy", -1)]
        vmem = pl.BlockSpec(memory_space=pltpu.VMEM)
        smem = pl.BlockSpec(memory_space=pltpu.SMEM)
        params = pltpu.CompilerParams(vmem_limit_bytes=48 * 1024 * 1024)
        f32 = jnp.float32
        mine = pl.pallas_call(
            pack_kernel,
            out_shape=jax.ShapeDtypeStruct((depth, KEPT, 2 * LANES), f32),
            in_specs=[vmem] * 3,
            out_specs=vmem,
            compiler_params=params,
        )(inner, *inner_sides)
        other = lax.ppermute(mine, "phys", [(0, 1), (1, 0)])
        rows = 5 * x_cells
        adjoint = pl.pallas_call(
            lambda *refs: smooth_kernel(depth_w, (x_peers, y_peers), *refs),
            out_shape=jax.ShapeDtypeStruct((6, depth, KEPT, 2 * LANES), f32),
            in_specs=[smem] * 2 + [vmem] * 6 + [pl.BlockSpec(memory_space=pl.ANY)] * 2,
            out_specs=vmem,
            scratch_shapes=[
                pltpu.VMEM((3, rows, 6 * LANES), f32),
                pltpu.VMEM((6, depth, ROWS, 2 * LANES), f32),
                pltpu.VMEM((6 * depth * ROWS, 5 * LANES), jnp.bfloat16),
                pltpu.VMEM((6 * depth * ROWS, 5 * LANES), jnp.bfloat16),
                pltpu.VMEM((3, depth, rows, LANES), f32),
                pltpu.VMEM(x_all.shape[1:], jnp.bfloat16),
                pltpu.VMEM(y_all.shape[1:], jnp.bfloat16),
                pltpu.SemaphoreType.DMA,
                pltpu.SemaphoreType.DMA,
            ],
            compiler_params=params,
            cost_estimate=pl.CostEstimate(
                flops=8 * 10**9, bytes_accessed=4 * 10**6, transcendentals=0
            ),
        )(
            which, channel_weight, inner_sides[0], inner, inner_sides[1],
            outer_sides[0], outer, outer_sides[1], x_all, y_all,
        )
        own, send = pl.pallas_call(
            gradient_kernel,
            out_shape=[jax.ShapeDtypeStruct(field.shape, f32)] * 2,
            in_specs=[vmem] * 3,
            out_specs=[vmem] * 2,
            compiler_params=params,
        )(adjoint, mine, other)
        got = lax.ppermute(send, "phys", [(0, 1), (1, 0)])
        return (own + got)[None]

    in_specs = (P("phys", None, "gx", "gy"), P())
    out_specs = P("phys", None, "gx", "gy")
    return jax.shard_map(shards, mesh=mesh, in_specs=in_specs, out_specs=out_specs, check_vma=False)
```

```python
import math

import jax
import jax.numpy as jnp
import ml_dtypes
import numpy as np
from jax import lax
from jax.experimental import pallas as pl
from jax.experimental.pallas import tpu as pltpu
from jax.sharding import PartitionSpec as P

DILATIONS = (1, 4)
TAPS = 15
LANES = 128
ROWS = 72


def taps():
    weights = np.array([math.exp(-k * k / 50.0) for k in range(-TAPS, TAPS + 1)])
    return weights / weights.sum()


def squared(length, dilation):
    matrix = np.zeros((length, length))
    for k, weight in zip(range(-TAPS, TAPS + 1), taps()):
        matrix += weight * np.eye(length, k=dilation * k)
    return matrix @ matrix


def window(matrix, row_ids, col_ids):
    count = matrix.shape[0]
    row_ok = (row_ids >= 0) & (row_ids < count)
    col_ok = (col_ids >= 0) & (col_ids < count)
    picked = matrix[np.clip(row_ids, 0, count - 1)][:, np.clip(col_ids, 0, count - 1)]
    return picked * row_ok[:, None] * col_ok[None, :]


def stored(tables, edge, axis):
    count = tables.shape[0]
    if count > 2 * edge + 1:
        tables = np.concatenate([tables[: edge + 1], tables[count - edge :]], 0)
    high = tables.astype(np.float32).astype(ml_dtypes.bfloat16)
    low = (tables - high.astype(np.float64)).astype(np.float32).astype(ml_dtypes.bfloat16)
    return jnp.asarray(np.concatenate([high, low, high] if axis == 2 else [high, high, low], axis))


def table_of(index, count, edge):
    if count <= 2 * edge + 1:
        return index
    return jnp.minimum(index, edge) + jnp.maximum(index - (count - 1 - edge), 0)


def split_f32(value):
    high = value.astype(jnp.bfloat16)
    low = (value - high.astype(jnp.float32)).astype(jnp.bfloat16)
    return high, low


def off_grid(count):
    return np.full(count, -1)


def x_tables(peers, block):
    tables = []
    matrices = [squared(peers * block, d) for d in DILATIONS]
    for i in range(peers):
        start = i * block
        out_ids = np.concatenate(
            [
                np.arange(start, start + block + 1),
                off_grid(ROWS - block - 2),
                [start - 1],
            ]
        )
        in_ids = np.arange(start - 2 * block, start + 3 * block)
        tables.append(np.concatenate([window(m, out_ids, in_ids) for m in matrices], 0))
    return np.stack(tables)


def y_tables(peers, block):
    tables = []
    fine, coarse = [squared(peers * block, d) for d in DILATIONS]
    for i in range(peers):
        start = i * block
        own = np.arange(start, start + block)
        left, right = own - block, own + block
        edge = np.concatenate([right[: block // 2], left[block // 2 :]])
        out_ids = np.concatenate(
            [own, [start + block], off_grid(block - 2), [start - 1]]
        )
        wide = np.concatenate([left, own, right])
        near = np.concatenate([own, edge])
        tables.append(
            np.concatenate(
                [window(coarse, out_ids, wide).T, window(fine, out_ids, near).T], 0
            )
        )
    return np.stack(tables)


def lane_index(shape):
    return lax.broadcasted_iota(jnp.int32, shape, len(shape) - 1)


def pack_kernel(near_ref, left_ref, right_ref, out_ref):
    block = out_ref.shape[1] - 8
    for z in range(out_ref.shape[0]):
        for column in range(2):
            def rows(at, count):
                if column == 0:
                    return near_ref[z, at : at + count, :]
                l = left_ref[z, at : at + count, :]
                r = right_ref[z, at : at + count, :]
                return jnp.where(lane_index(l.shape) < LANES // 2, r, l)

            after, before = rows(2 * block, 8), rows(block - 8, 8)
            sub = lax.broadcasted_iota(jnp.int32, after.shape, 0)
            lanes = slice(column * LANES, (column + 1) * LANES)
            out_ref[z, 0:block, lanes] = rows(block, block)
            out_ref[z, block : block + 8, lanes] = jnp.where(sub < 4, after, before)


def smooth_kernel(
    depth_w, counts, which_ref, weight_ref, *refs
):
    inner_refs, outer_refs, refs = refs[:3], refs[3:6], refs[6:]
    x_all, y_all, out_ref, slope_ref, near_ref, high_ref, low_ref, ext_ref, x_ref, y_ref, x_sem, y_sem = refs
    blocks, depth, rows, _ = ext_ref.shape
    chunk = 32
    x_copy = pltpu.make_async_copy(x_all.at[table_of(which_ref[0], counts[0], 2)], x_ref, x_sem)
    y_copy = pltpu.make_async_copy(y_all.at[table_of(which_ref[1], counts[1], 1)], y_ref, y_sem)
    x_copy.start()
    y_copy.start()
    side = rows // 5
    for b in range(blocks):
        for z in range(depth):
            ext_ref[b, z, side : 4 * side] = inner_refs[b][z]
            ext_ref[b, z, :side] = outer_refs[b][z, :side]
            ext_ref[b, z, 4 * side :] = outer_refs[b][z, side:]
    x_copy.wait()
    centre = float(depth_w[1][0][0])

    for pair in range(depth // 2):
        for k in range(2):
            z = 2 * pair + k
            for b in range(3):
                lanes = slice((3 * k + b) * LANES, (3 * k + b + 1) * LANES)
                for r in range(0, rows, chunk):
                    at = slice(r, r + chunk)
                    mid = ext_ref[b, z, at, :]
                    if r == 0:
                        before = jnp.concatenate([mid[:1], mid[:-1]], 0)
                    else:
                        before = ext_ref[b, z, r - 1 : r + chunk - 1, :]
                    if r + chunk == rows:
                        after = jnp.concatenate([mid[1:], mid[-1:]], 0)
                    else:
                        after = ext_ref[b, z, r + 1 : r + chunk + 1, :]
                    slope_ref[0, at, lanes] = 0.5 * (after - before)
                    lane = lane_index(mid.shape)
                    prev, nxt = pltpu.roll(mid, 1, 1), pltpu.roll(mid, LANES - 1, 1)
                    if b > 0:
                        prev = jnp.where(lane == 0, pltpu.roll(ext_ref[b - 1, z, at, :], 1, 1), prev)
                    if b < 2:
                        nxt = jnp.where(
                            lane == LANES - 1, pltpu.roll(ext_ref[b + 1, z, at, :], LANES - 1, 1), nxt
                        )
                    slope_ref[1, at, lanes] = 0.5 * (nxt - prev)
                    above = ext_ref[b, z + 1, at, :] if z + 1 < depth else jnp.zeros_like(mid)
                    below = ext_ref[b, z - 1, at, :] if z > 0 else jnp.zeros_like(mid)
                    slope_ref[2, at, lanes] = 0.5 * (above - below)
        for c, (i, j) in enumerate(((0, 0), (1, 1), (2, 2), (0, 1), (0, 2), (1, 2))):
            high, low = split_f32(slope_ref[i] * slope_ref[j])
            done = jnp.dot(
                x_ref[...],
                jnp.concatenate([high, high, low], 0),
                preferred_element_type=jnp.float32,
            )
            fine, coarse = done[:ROWS], done[ROWS:] * (weight_ref[1, c] * centre)
            at = slice((2 * c + pair) * 2 * ROWS, (2 * c + pair + 1) * 2 * ROWS)
            wide = jnp.concatenate([coarse[:, : 3 * LANES], coarse[:, 3 * LANES :]], 0)
            high_ref[at, : 3 * LANES], low_ref[at, : 3 * LANES] = split_f32(wide)
            for k in range(2):
                z = 2 * pair + k
                l, o, r = [
                    fine[:, (3 * k + b) * LANES : (3 * k + b + 1) * LANES] for b in range(3)
                ]
                near_ref[c, z, :, :LANES] = o
                near_ref[c, z, :, LANES:] = jnp.where(lane_index(l.shape) < LANES // 2, r, l)
    y_copy.wait()
    for c in range(6):
        planes = [near_ref[c, z] * weight_ref[0, c] for z in range(depth)]
        for pair in range(depth // 2):
            mixed = []
            for z in (2 * pair, 2 * pair + 1):
                row = [float(w) for w in depth_w[0][z]]
                mixed.append(sum(planes[k] * row[k] for k in range(1, depth)) + planes[0] * row[0])
            at = slice((2 * c + pair) * 2 * ROWS, (2 * c + pair + 1) * 2 * ROWS)
            high_ref[at, 3 * LANES :], low_ref[at, 3 * LANES :] = split_f32(
                jnp.concatenate(mixed, 0)
            )
        at = slice(c * depth * ROWS, (c + 1) * depth * ROWS)
        high, low = high_ref[at, :], low_ref[at, :]
        done = jnp.dot(
            jnp.concatenate([high, low, high], 1),
            y_ref[...],
            preferred_element_type=jnp.float32,
        )
        for z in range(depth):
            out_ref[c, z] = done[z * ROWS : (z + 1) * ROWS]


def gradient_kernel(sign, adj_ref, model, result):
    depth, rows, cols = model.shape
    block = result.shape[1]
    q_z = []
    total = []
    for z in range(depth):
        m = model[z]
        s_x = 0.5 * (pltpu.roll(m, rows - 1, 0) - pltpu.roll(m, 1, 0))
        s_y = 0.5 * (pltpu.roll(m, cols - 1, 1) - pltpu.roll(m, 1, 1))
        above = model[z + 1] if z + 1 < depth else jnp.zeros_like(m)
        below = model[z - 1] if z > 0 else jnp.zeros_like(m)
        s_z = 0.5 * (above - below)
        a = [adj_ref[c, z] for c in range(6)]
        q_x = 2.0 * a[0] * s_x + a[3] * s_y + a[4] * s_z
        q_y = 2.0 * a[1] * s_y + a[3] * s_x + a[5] * s_z
        q_z.append((2.0 * a[2] * s_z + a[4] * s_x + a[5] * s_y)[:block, :LANES])
        lateral = pltpu.roll(q_x, 1, 0) - pltpu.roll(q_x, rows - 1, 0)
        lateral = lateral + pltpu.roll(q_y, 1, 1) - pltpu.roll(q_y, cols - 1, 1)
        total.append(lateral[:block, :LANES])
    for z in range(depth):
        value = total[z]
        if z > 0:
            value = value + q_z[z - 1]
        if z + 1 < depth:
            value = value - q_z[z + 1]
        result[z] = sign * value


def swap_columns(value, first):
    peers = lax.axis_size("gy")
    route = []
    for i in range(first, peers - 1, 2):
        route += [(i, i + 1), (i + 1, i)]
    return lax.ppermute(value, "gy", route)


def shift(value, axis, step):
    peers = lax.axis_size(axis)
    route = [(i, i + step) for i in range(peers) if 0 <= i + step < peers]
    return lax.ppermute(value, axis, route)


def solution(mesh):
    x_peers, y_peers = mesh.shape["gx"], mesh.shape["gy"]

    def shards(models, channel_weight):
        field = models[0]
        depth, x_cells, y_cells = field.shape
        depth_w = [squared(depth, d).tolist() for d in DILATIONS]
        x_index, y_index = lax.axis_index("gx"), lax.axis_index("gy")
        x_all = stored(x_tables(x_peers, x_cells), 2, 2)
        y_all = stored(y_tables(y_peers, y_cells), 1, 1)
        which = jnp.stack([x_index, y_index])
        near = [shift(field, "gx", 1), shift(field, "gx", -1)]
        far = [shift(field, "gx", 2), shift(field, "gx", -2)]
        inner = jnp.concatenate([near[0], field, near[1]], 1)
        inner_sides = [shift(inner, "gy", 1), shift(inner, "gy", -1)]
        outer = jnp.concatenate(far, 1)
        outer_sides = [shift(outer, "gy", 1), shift(outer, "gy", -1)]
        vmem = pl.BlockSpec(memory_space=pltpu.VMEM)
        smem = pl.BlockSpec(memory_space=pltpu.SMEM)
        params = pltpu.CompilerParams(vmem_limit_bytes=48 * 1024 * 1024)
        f32 = jnp.float32
        mine = pl.pallas_call(
            pack_kernel,
            out_shape=jax.ShapeDtypeStruct((depth, ROWS, 2 * LANES), f32),
            in_specs=[vmem] * 3,
            out_specs=vmem,
            compiler_params=params,
        )(inner, *inner_sides)
        other = lax.ppermute(mine, "phys", [(0, 1), (1, 0)])
        rows = 5 * x_cells
        adjoint = pl.pallas_call(
            lambda *refs: smooth_kernel(depth_w, (x_peers, y_peers), *refs),
            out_shape=jax.ShapeDtypeStruct((6, depth, ROWS, 2 * LANES), f32),
            in_specs=[smem] * 2 + [vmem] * 6 + [pl.BlockSpec(memory_space=pl.ANY)] * 2,
            out_specs=vmem,
            scratch_shapes=[
                pltpu.VMEM((3, rows, 6 * LANES), f32),
                pltpu.VMEM((6, depth, ROWS, 2 * LANES), f32),
                pltpu.VMEM((6 * depth * ROWS, 5 * LANES), jnp.bfloat16),
                pltpu.VMEM((6 * depth * ROWS, 5 * LANES), jnp.bfloat16),
                pltpu.VMEM((3, depth, rows, LANES), f32),
                pltpu.VMEM(x_all.shape[1:], jnp.bfloat16),
                pltpu.VMEM(y_all.shape[1:], jnp.bfloat16),
                pltpu.SemaphoreType.DMA,
                pltpu.SemaphoreType.DMA,
            ],
            compiler_params=params,
            cost_estimate=pl.CostEstimate(
                flops=8 * 10**9, bytes_accessed=4 * 10**6, transcendentals=0
            ),
        )(
            which, channel_weight, inner_sides[0], inner, inner_sides[1],
            outer_sides[0], outer, outer_sides[1], x_all, y_all,
        )
        def gradient(sign, model):
            return pl.pallas_call(
                lambda *refs: gradient_kernel(sign, *refs),
                out_shape=jax.ShapeDtypeStruct(field.shape, f32),
                in_specs=[vmem] * 2,
                out_specs=vmem,
                compiler_params=params,
                cost_estimate=pl.CostEstimate(
                    flops=10**7, bytes_accessed=2 * 10**6, transcendentals=0
                ),
            )(adjoint, model)

        got = lax.ppermute(gradient(-0.5, other), "phys", [(0, 1), (1, 0)])
        return (gradient(0.5, mine) + got)[None]

    in_specs = (P("phys", None, "gx", "gy"), P())
    out_specs = P("phys", None, "gx", "gy")
    return jax.shard_map(shards, mesh=mesh, in_specs=in_specs, out_specs=out_specs, check_vma=False)
```

```python
import math

import jax
import jax.numpy as jnp
import ml_dtypes
import numpy as np
from jax import lax
from jax.experimental import pallas as pl
from jax.experimental.pallas import tpu as pltpu
from jax.sharding import PartitionSpec as P

DILATIONS = (1, 4)
TAPS = 15
LANES = 128
ROWS = 72


def taps():
    weights = np.array([math.exp(-k * k / 50.0) for k in range(-TAPS, TAPS + 1)])
    return weights / weights.sum()


def squared(length, dilation):
    matrix = np.zeros((length, length))
    for k, weight in zip(range(-TAPS, TAPS + 1), taps()):
        matrix += weight * np.eye(length, k=dilation * k)
    return matrix @ matrix


def window(matrix, row_ids, col_ids):
    count = matrix.shape[0]
    row_ok = (row_ids >= 0) & (row_ids < count)
    col_ok = (col_ids >= 0) & (col_ids < count)
    picked = matrix[np.clip(row_ids, 0, count - 1)][:, np.clip(col_ids, 0, count - 1)]
    return picked * row_ok[:, None] * col_ok[None, :]


def stored(tables, edge, axis):
    count = tables.shape[0]
    if count > 2 * edge + 1:
        tables = np.concatenate([tables[: edge + 1], tables[count - edge :]], 0)
    high = tables.astype(np.float32).astype(ml_dtypes.bfloat16)
    low = (tables - high.astype(np.float64)).astype(np.float32).astype(ml_dtypes.bfloat16)
    return jnp.asarray(np.concatenate([high, low, high] if axis == 2 else [high, high, low], axis))


def table_of(index, count, edge):
    if count <= 2 * edge + 1:
        return index
    return jnp.minimum(index, edge) + jnp.maximum(index - (count - 1 - edge), 0)


def split_f32(value):
    high = value.astype(jnp.bfloat16)
    low = (value - high.astype(jnp.float32)).astype(jnp.bfloat16)
    return high, low


def off_grid(count):
    return np.full(count, -1)


def x_tables(peers, block):
    tables = []
    matrices = [squared(peers * block, d) for d in DILATIONS]
    for i in range(peers):
        start = i * block
        out_ids = np.concatenate(
            [
                np.arange(start, start + block + 1),
                off_grid(ROWS - block - 2),
                [start - 1],
            ]
        )
        in_ids = np.arange(start - 2 * block, start + 3 * block)
        tables.append(np.concatenate([window(m, out_ids, in_ids) for m in matrices], 0))
    return np.stack(tables)


def y_tables(peers, block):
    tables = []
    fine, coarse = [squared(peers * block, d) for d in DILATIONS]
    for i in range(peers):
        start = i * block
        own = np.arange(start, start + block)
        left, right = own - block, own + block
        edge = np.concatenate([right[: block // 2], left[block // 2 :]])
        out_ids = np.concatenate(
            [own, [start + block], off_grid(block - 2), [start - 1]]
        )
        wide = np.concatenate([left, own, right])
        near = np.concatenate([own, edge])
        tables.append(
            np.concatenate(
                [window(coarse, out_ids, wide).T, window(fine, out_ids, near).T], 0
            )
        )
    return np.stack(tables)


def lane_index(shape):
    return lax.broadcasted_iota(jnp.int32, shape, len(shape) - 1)


def pack_kernel(near_ref, left_ref, right_ref, out_ref):
    block = out_ref.shape[1] - 8
    for z in range(out_ref.shape[0]):
        for column in range(2):
            def rows(at, count):
                if column == 0:
                    return near_ref[z, at : at + count, :]
                l = left_ref[z, at : at + count, :]
                r = right_ref[z, at : at + count, :]
                return jnp.where(lane_index(l.shape) < LANES // 2, r, l)

            after, before = rows(2 * block, 8), rows(block - 8, 8)
            sub = lax.broadcasted_iota(jnp.int32, after.shape, 0)
            lanes = slice(column * LANES, (column + 1) * LANES)
            out_ref[z, 0:block, lanes] = rows(block, block)
            out_ref[z, block : block + 8, lanes] = jnp.where(sub < 4, after, before)


def smooth_kernel(
    depth_w, counts, which_ref, weight_ref, *refs
):
    inner_refs, outer_refs, refs = refs[:3], refs[3:6], refs[6:]
    x_all, y_all, out_ref, slope_ref, near_ref, high_ref, low_ref, ext_ref, x_ref, y_ref, x_sem, y_sem = refs
    blocks, depth, rows, _ = ext_ref.shape
    chunk = 32
    x_copy = pltpu.make_async_copy(x_all.at[table_of(which_ref[0], counts[0], 2)], x_ref, x_sem)
    y_copy = pltpu.make_async_copy(y_all.at[table_of(which_ref[1], counts[1], 1)], y_ref, y_sem)
    x_copy.start()
    y_copy.start()
    side = rows // 5
    for b in range(blocks):
        for z in range(depth):
            ext_ref[b, z, side : 4 * side] = inner_refs[b][z]
            ext_ref[b, z, :side] = outer_refs[b][z, :side]
            ext_ref[b, z, 4 * side :] = outer_refs[b][z, side:]
    x_copy.wait()
    centre = float(depth_w[1][0][0])

    for pair in range(depth // 2):
        for k in range(2):
            z = 2 * pair + k
            for b in range(3):
                lanes = slice((3 * k + b) * LANES, (3 * k + b + 1) * LANES)
                for r in range(0, rows, chunk):
                    at = slice(r, r + chunk)
                    mid = ext_ref[b, z, at, :]
                    if r == 0:
                        before = jnp.concatenate([mid[:1], mid[:-1]], 0)
                    else:
                        before = ext_ref[b, z, r - 1 : r + chunk - 1, :]
                    if r + chunk == rows:
                        after = jnp.concatenate([mid[1:], mid[-1:]], 0)
                    else:
                        after = ext_ref[b, z, r + 1 : r + chunk + 1, :]
                    slope_ref[0, at, lanes] = 0.5 * (after - before)
                    lane = lane_index(mid.shape)
                    prev, nxt = pltpu.roll(mid, 1, 1), pltpu.roll(mid, LANES - 1, 1)
                    if b > 0:
                        prev = jnp.where(lane == 0, pltpu.roll(ext_ref[b - 1, z, at, :], 1, 1), prev)
                    if b < 2:
                        nxt = jnp.where(
                            lane == LANES - 1, pltpu.roll(ext_ref[b + 1, z, at, :], LANES - 1, 1), nxt
                        )
                    slope_ref[1, at, lanes] = 0.5 * (nxt - prev)
                    above = ext_ref[b, z + 1, at, :] if z + 1 < depth else jnp.zeros_like(mid)
                    below = ext_ref[b, z - 1, at, :] if z > 0 else jnp.zeros_like(mid)
                    slope_ref[2, at, lanes] = 0.5 * (above - below)
        for c, (i, j) in enumerate(((0, 0), (1, 1), (2, 2), (0, 1), (0, 2), (1, 2))):
            high, low = split_f32(slope_ref[i] * slope_ref[j])
            done = jnp.dot(
                x_ref[...],
                jnp.concatenate([high, high, low], 0),
                preferred_element_type=jnp.float32,
            )
            fine, coarse = done[:ROWS], done[ROWS:] * (weight_ref[1, c] * centre)
            at = slice((2 * c + pair) * 2 * ROWS, (2 * c + pair + 1) * 2 * ROWS)
            wide = jnp.concatenate([coarse[:, : 3 * LANES], coarse[:, 3 * LANES :]], 0)
            high_ref[at, : 3 * LANES], low_ref[at, : 3 * LANES] = split_f32(wide)
            for k in range(2):
                z = 2 * pair + k
                l, o, r = [
                    fine[:, (3 * k + b) * LANES : (3 * k + b + 1) * LANES] for b in range(3)
                ]
                near_ref[c, z, :, :LANES] = o
                near_ref[c, z, :, LANES:] = jnp.where(lane_index(l.shape) < LANES // 2, r, l)
    y_copy.wait()
    for c in range(6):
        planes = [near_ref[c, z] * weight_ref[0, c] for z in range(depth)]
        for pair in range(depth // 2):
            mixed = []
            for z in (2 * pair, 2 * pair + 1):
                row = [float(w) for w in depth_w[0][z]]
                mixed.append(sum(planes[k] * row[k] for k in range(1, depth)) + planes[0] * row[0])
            at = slice((2 * c + pair) * 2 * ROWS, (2 * c + pair + 1) * 2 * ROWS)
            high_ref[at, 3 * LANES :], low_ref[at, 3 * LANES :] = split_f32(
                jnp.concatenate(mixed, 0)
            )
        at = slice(c * depth * ROWS, (c + 1) * depth * ROWS)
        high, low = high_ref[at, :], low_ref[at, :]
        done = jnp.dot(
            jnp.concatenate([high, low, high], 1),
            y_ref[...],
            preferred_element_type=jnp.float32,
        )
        for z in range(depth):
            out_ref[c, z] = done[z * ROWS : (z + 1) * ROWS]


def gradient_kernel(sign, adj_ref, model, result):
    depth, rows, cols = model.shape
    block = result.shape[1]
    q_z = []
    total = []
    for z in range(depth):
        m = model[z]
        s_x = 0.5 * (pltpu.roll(m, rows - 1, 0) - pltpu.roll(m, 1, 0))
        s_y = 0.5 * (pltpu.roll(m, cols - 1, 1) - pltpu.roll(m, 1, 1))
        above = model[z + 1] if z + 1 < depth else jnp.zeros_like(m)
        below = model[z - 1] if z > 0 else jnp.zeros_like(m)
        s_z = 0.5 * (above - below)
        a = [adj_ref[c, z] for c in range(6)]
        q_x = 2.0 * a[0] * s_x + a[3] * s_y + a[4] * s_z
        q_y = 2.0 * a[1] * s_y + a[3] * s_x + a[5] * s_z
        q_z.append((2.0 * a[2] * s_z + a[4] * s_x + a[5] * s_y)[:block, :LANES])
        lateral = pltpu.roll(q_x, 1, 0) - pltpu.roll(q_x, rows - 1, 0)
        lateral = lateral + pltpu.roll(q_y, 1, 1) - pltpu.roll(q_y, cols - 1, 1)
        total.append(lateral[:block, :LANES])
    for z in range(depth):
        value = total[z]
        if z > 0:
            value = value + q_z[z - 1]
        if z + 1 < depth:
            value = value - q_z[z + 1]
        result[z] = sign * value


def swap_columns(value, first):
    peers = lax.axis_size("gy")
    route = []
    for i in range(first, peers - 1, 2):
        route += [(i, i + 1), (i + 1, i)]
    return lax.ppermute(value, "gy", route)


def shift(value, axis, step):
    peers = lax.axis_size(axis)
    route = [(i, i + step) for i in range(peers) if 0 <= i + step < peers]
    return lax.ppermute(value, axis, route)


def solution(mesh):
    x_peers, y_peers = mesh.shape["gx"], mesh.shape["gy"]

    def shards(models, channel_weight):
        field = models[0]
        depth, x_cells, y_cells = field.shape
        depth_w = [squared(depth, d).tolist() for d in DILATIONS]
        x_index, y_index = lax.axis_index("gx"), lax.axis_index("gy")
        x_all = stored(x_tables(x_peers, x_cells), 2, 2)
        y_all = stored(y_tables(y_peers, y_cells), 1, 1)
        which = jnp.stack([x_index, y_index])
        near = [shift(field, "gx", 1), shift(field, "gx", -1)]
        far = [shift(field, "gx", 2), shift(field, "gx", -2)]
        inner = jnp.concatenate([near[0], field, near[1]], 1)
        inner_sides = [shift(inner, "gy", 1), shift(inner, "gy", -1)]
        outer = jnp.concatenate(far, 1)
        outer_sides = [shift(outer, "gy", 1), shift(outer, "gy", -1)]
        vmem = pl.BlockSpec(memory_space=pltpu.VMEM)
        smem = pl.BlockSpec(memory_space=pltpu.SMEM)
        params = pltpu.CompilerParams(vmem_limit_bytes=48 * 1024 * 1024)
        f32 = jnp.float32
        mine = pl.pallas_call(
            pack_kernel,
            out_shape=jax.ShapeDtypeStruct((depth, ROWS, 2 * LANES), f32),
            in_specs=[vmem] * 3,
            out_specs=vmem,
            compiler_params=params,
        )(inner, *inner_sides)
        other = lax.ppermute(mine, "phys", [(0, 1), (1, 0)])
        rows = 5 * x_cells
        adjoint = pl.pallas_call(
            lambda *refs: smooth_kernel(depth_w, (x_peers, y_peers), *refs),
            out_shape=jax.ShapeDtypeStruct((6, depth, ROWS, 2 * LANES), f32),
            in_specs=[smem] * 2 + [vmem] * 6 + [pl.BlockSpec(memory_space=pl.ANY)] * 2,
            out_specs=vmem,
            scratch_shapes=[
                pltpu.VMEM((3, rows, 6 * LANES), f32),
                pltpu.VMEM((6, depth, ROWS, 2 * LANES), f32),
                pltpu.VMEM((6 * depth * ROWS, 5 * LANES), jnp.bfloat16),
                pltpu.VMEM((6 * depth * ROWS, 5 * LANES), jnp.bfloat16),
                pltpu.VMEM((3, depth, rows, LANES), f32),
                pltpu.VMEM(x_all.shape[1:], jnp.bfloat16),
                pltpu.VMEM(y_all.shape[1:], jnp.bfloat16),
                pltpu.SemaphoreType.DMA,
                pltpu.SemaphoreType.DMA,
            ],
            compiler_params=params,
            cost_estimate=pl.CostEstimate(
                flops=8 * 10**9, bytes_accessed=4 * 10**6, transcendentals=0
            ),
        )(
            which, channel_weight, inner_sides[0], inner, inner_sides[1],
            outer_sides[0], outer, outer_sides[1], x_all, y_all,
        )
        def gradient(sign, model):
            return pl.pallas_call(
                lambda *refs: gradient_kernel(sign, *refs),
                out_shape=jax.ShapeDtypeStruct(field.shape, f32),
                in_specs=[vmem] * 2,
                out_specs=vmem,
                compiler_params=params,
                cost_estimate=pl.CostEstimate(
                    flops=10**7, bytes_accessed=2 * 10**6, transcendentals=0
                ),
            )(adjoint, model)

        both = lax.all_gather(gradient(-0.5, other), "phys")
        got = jnp.where(lax.axis_index("phys") == 0, both[1], both[0])
        return (gradient(0.5, mine) + got)[None]

    in_specs = (P("phys", None, "gx", "gy"), P())
    out_specs = P("phys", None, "gx", "gy")
    return jax.shard_map(shards, mesh=mesh, in_specs=in_specs, out_specs=out_specs, check_vma=False)
```
